32 devices in a mesh: depth: 8 (over z, y), tile: 4 (over x, core).
Axes of the slice: x: 2, y: 2, z: 4, core: 2. Of those that a mesh axis runs over, the one named last changes fastest.
Arguments:
- density: float32 [16, 512, 2048], P('depth', 'tile'), may hold values from -6 to 6
- bins: int32 [16, 512, 2048], P('depth', 'tile'), may hold values from 0 to 255
- colors: bfloat16 [3, 256], replicated, may hold values from 0.099609375 to 1
- extinction: bfloat16 [256], replicated, may hold values from 0.049804688 to 20
Outputs:
- image: float32 [4, 512, 2048], P(None, 'tile', 'depth')
The draws below stay inside these ranges and needn't reach their ends.
All inputs are finite; a program needn't handle non-finite values.
Results may differ from the reference program's by a relative error of at most 0.0003.
Values sent between devices are 32-bit elements; how exact they have to be, the bound alone decides.
No kernel may reach another device: no remote copies, remote signals or barrier semaphores. Data moves between devices by JAX's collectives and lax.ppermute only.
A program may use at most 256 MiB of HBM per device.

```python
import math
import jax
import jax.numpy as jnp
import numpy as np
from jax import lax

NZ = 2048
BINS = 256
NX = 16
NY = 512
SLABS = 8


def with_ends(values, rng, low, largest):
    longest = values.shape.index(max(values.shape))
    spots = []
    for shift in (0, 1):
        where = [jax.random.randint(jax.random.fold_in(rng, axis), (), 0, length) for axis, length in enumerate(values.shape)]
        where[longest] = (where[longest] + shift) % values.shape[longest]
        spots.append(tuple(where))
    return values.at[spots[0]].set(low).at[spots[1]].set(largest)


def shard_levels(key, extent, shards, smallest, high):
    def one(dim, shards_of):
        heights = jax.random.uniform(jax.random.fold_in(jax.random.fold_in(key, 6), dim), (shards_of,), jnp.float32, smallest / len(shards), high / len(shards))
        return jnp.repeat(jnp.exp(heights), extent[dim] // shards_of).reshape((-1,) + (1,) * (len(extent) - dim - 1))

    level = one(*shards[0])
    for cut in shards[1:]:
        level = level * one(*cut)
    return level


def bell_draw(stream_key, dims, spread, most, pieces=(), held_as=jnp.bfloat16):
    values = jax.random.normal(stream_key, dims, jnp.float32) * spread
    if len(pieces) > 0:
        values = shard_levels(stream_key, dims, pieces, -0.22, 0.18) * values
    return jnp.clip(values, min=-most, max=most).astype(held_as)


def setup_inputs(seed: int = 0) -> dict:
    seeds = jax.random.split(jax.random.key(seed), 5)
    density = bell_draw(seeds[0], (NX, NY, NZ), 1.0, 6.0, ((0, 8), (1, 4)), jnp.float32)
    bins = with_ends(jax.random.randint(seeds[1], (NX, NY, NZ), 0, BINS), jax.random.fold_in(seeds[1], 1), 0, BINS - 1).astype(jnp.int32)
    colors = jnp.clip(jax.random.uniform(seeds[2], (3, BINS), jnp.float32, 0.099609375, 1.0), 0.099609375, 1.0).astype(jnp.bfloat16)
    extinction = jnp.clip(jnp.exp(jax.random.uniform(seeds[3], (BINS,), jnp.float32, math.log(0.049804688), math.log(20.0))), 0.049804688, 20.0).astype(jnp.bfloat16)
    return dict(density=density, bins=bins, colors=colors, extinction=extinction)


def reversed_order(count):
    width_bits = count.bit_length() - 1
    result = []
    for index_j in range(count):
        value = 0
        for shift_k in range(width_bits):
            value = value | (index_j >> shift_k & 1) << width_bits - 1 - shift_k
        result.append(value)
    return np.array(result, dtype=np.int32)

def reference(density, bins, colors, extinction):
    lookup = jnp.concatenate([colors.astype(jnp.float32), extinction.astype(jnp.float32)[None, :]], 0)
    depth_scale = 0.6 / NX
    padded = jnp.pad(density, ((1, 1), (0, 0), (0, 0)))

    def plane_step(carry, index_x):
        radiance, running = carry
        before = lax.dynamic_slice_in_dim(padded, index_x, 1, 0)[0]
        center = lax.dynamic_slice_in_dim(padded, index_x + 1, 1, 0)[0]
        after = lax.dynamic_slice_in_dim(padded, index_x + 2, 1, 0)[0]
        grad_x = (after - before) * 0.5
        row_pad = jnp.pad(center, ((1, 1), (0, 0)))
        grad_y = (row_pad[2:] - row_pad[:-2]) * 0.5
        col_pad = jnp.pad(center, ((0, 0), (1, 1)))
        grad_z = (col_pad[:, 2:] - col_pad[:, :-2]) * 0.5
        lit = jnp.abs(0.48 * grad_x + 0.6 * grad_y + 0.64 * grad_z)
        shade = 0.3 + 0.7 * lit / jnp.sqrt(grad_x * grad_x + grad_y * grad_y + grad_z * grad_z + 1.0)
        plane_bins = lax.dynamic_slice_in_dim(bins, index_x, 1, 0)[0]
        entries = jnp.take(lookup, plane_bins, axis=1)
        optical = entries[3] * depth_scale
        emitted = entries[:3] * shade * (1.0 - jnp.exp(-optical))
        radiance = radiance + jnp.exp(-running) * emitted
        running = running + optical
        return ((radiance, running), None)
    start = (jnp.zeros((3, NY, NZ), jnp.float32), jnp.zeros((NY, NZ), jnp.float32))
    (radiance, running), unused = lax.scan(plane_step, start, jnp.arange(NX, dtype=jnp.int32))
    full = jnp.concatenate([radiance, (1.0 - jnp.exp(-running))[None]], 0)
    blocks = full.reshape(4, NY, SLABS, NZ // SLABS)
    blocks = blocks[:, :, reversed_order(SLABS), :]
    return blocks.reshape(4, NY, NZ)
```

```python
import functools

import jax
import jax.numpy as jnp
from jax import lax
from jax.experimental import pallas as pl
from jax.experimental.pallas import tpu as pltpu
from jax.sharding import PartitionSpec as P

LANES = 128
VMEM_LIMIT = 24 * 1024 * 1024


def params():
    return pltpu.CompilerParams(vmem_limit_bytes=VMEM_LIMIT)


def pack_body(layers, rows, top_row, bottom_row, side_ref, dens, top, bottom, column, bins, out):
    side = side_ref[0]
    for layer in range(layers):
        out[layer * rows : (layer + 1) * rows, :] = dens[layer]
        out[(layers + layer) * rows : (layers + layer + 1) * rows, :] = bins[layer].astype(jnp.float32)
    base = 2 * layers * rows
    for layer in range(layers):
        out[base + 2 * layer : base + 2 * layer + 1, :] = top[layer, top_row : top_row + 1, :]
        out[base + 2 * layer + 1 : base + 2 * layer + 2, :] = bottom[layer, bottom_row : bottom_row + 1, :]
    lane = lax.broadcasted_iota(jnp.int32, (8, LANES), 1)
    edges = jnp.zeros((8, LANES), jnp.float32)
    for layer in range(layers):
        for step in range(rows // 8):
            block = column[layer, step * 8 : step * 8 + 8, :]
            edge = jnp.where(side == 0, block[:, LANES - 1 :], block[:, :1])
            edges = jnp.where(lane == layer * (rows // 8) + step, edge, edges)
    out[base + 4 : base + 8, :] = jnp.zeros((4, out.shape[1]), jnp.float32)
    out[base + 4 : base + 8, :LANES] = edges[:4]
    out[base + 4 : base + 8, LANES : 2 * LANES] = edges[4:]


def render_body(layers, rows, scale, top_row, bottom_row, side_ref, table, dens, top, bottom, column, bins, message, direct, passed, kept, sent, cells, ends, entry, rgbt, lookup):
    side = side_ref[0]
    bit = side_ref[1]
    half = dens.shape[2]
    tiles = half // LANES
    deep = 2 * layers
    mine = side * layers
    other = (1 - side) * layers
    base = 2 * layers * rows
    transmit = jnp.exp(table[3:4, :] * (-scale))
    for channel in range(4):
        value = table[channel : channel + 1, :] * (1.0 - transmit) if channel < 3 else transmit
        for part in range(2):
            lookup[2 * channel + part] = jnp.broadcast_to(value[:, part * LANES : (part + 1) * LANES], (8, LANES))
    body = pl.ds(8, rows)
    cells[(1 - side) * (deep + 1), body, :] = direct[...]
    cells[side * (deep + 1), body, :] = passed[...]
    low = message[base : base + 8, :LANES]
    high = message[base : base + 8, LANES : 2 * LANES]
    edges = jnp.concatenate([low[4:], high[4:]], 0)
    ends[side] = jnp.zeros_like(ends[side])
    for layer in range(layers):
        cells[1 + mine + layer, body, :] = dens[layer]
        cells[1 + mine + layer, 7:8, :] = top[layer, top_row : top_row + 1, :]
        cells[1 + mine + layer, 8 + rows : 9 + rows, :] = bottom[layer, bottom_row : bottom_row + 1, :]
        cells[1 + other + layer, body, :] = message[layer * rows : (layer + 1) * rows, :]
        cells[1 + other + layer, 7:8, :] = message[base + 2 * layer : base + 2 * layer + 1, :]
        cells[1 + other + layer, 8 + rows : 9 + rows, :] = message[base + 2 * layer + 1 : base + 2 * layer + 2, :]
        entry[mine + layer] = bins[layer]
        entry[other + layer] = message[(layers + layer) * rows : (layers + layer + 1) * rows, :].astype(jnp.int32)
        ends[1 - side, mine + layer] = column[layer]
        for step in range(rows // 8):
            place = layer * (rows // 8) + step
            ends[1 - side, other + layer, step * 8 : step * 8 + 8, :] = jnp.broadcast_to(edges[:, place : place + 1], (8, LANES))
    lane = lax.broadcasted_iota(jnp.int32, (8, LANES), 1)
    line = lax.broadcasted_iota(jnp.int32, (8, LANES), 0)

    def strip(step, carry):
        row = pl.multiple_of(step * 8, 8)
        here = pl.ds(row, 8)

        def tile_of(layer, tile):
            if tile < 0:
                return ends[0, layer, here, :]
            if tile == tiles:
                return ends[1, layer, here, :]
            return cells[1 + layer, pl.ds(row + 8, 8), tile * LANES : (tile + 1) * LANES]

        for tile in range(tiles):
            span = slice(tile * LANES, (tile + 1) * LANES)
            through = None
            total = None
            for layer in range(deep):
                before = cells[layer, pl.ds(row + 8, 8), span]
                after = cells[layer + 2, pl.ds(row + 8, 8), span]
                cell = tile_of(layer, tile)
                above = pltpu.roll(jnp.where(line == 7, cells[1 + layer, here, span], cell), 1, 0)
                below = pltpu.roll(jnp.where(line == 0, cells[1 + layer, pl.ds(row + 16, 8), span], cell), 7, 0)
                left = pltpu.roll(jnp.where(lane == LANES - 1, tile_of(layer, tile - 1), cell), 1, 1)
                right = pltpu.roll(jnp.where(lane == 0, tile_of(layer, tile + 1), cell), LANES - 1, 1)
                gx = after - before
                gy = below - above
                gz = right - left
                lit = jnp.abs(0.336 * gx + 0.42 * gy + 0.448 * gz)
                shade = 0.3 + lit * lax.rsqrt(gx * gx + gy * gy + gz * gz + 4.0)
                index = entry[layer, here, span]
                low_index = index & (LANES - 1)
                upper = index >= LANES
                looked = []
                for channel in range(4):
                    first = jnp.take_along_axis(lookup[2 * channel], low_index, axis=1, mode="promise_in_bounds")
                    second = jnp.take_along_axis(lookup[2 * channel + 1], low_index, axis=1, mode="promise_in_bounds")
                    looked.append(jnp.where(upper, second, first))
                if layer == 0:
                    total = [shade * looked[c] for c in range(3)]
                    through = looked[3]
                else:
                    weight = through * shade
                    total = [total[c] + weight * looked[c] for c in range(3)]
                    through = through * looked[3]
            which = jnp.where(bit == 0, tile // (tiles // 2), 1 - tile // (tiles // 2))
            place = slice((tile % (tiles // 2)) * LANES, (tile % (tiles // 2) + 1) * LANES)
            for c, value in enumerate(total + [through]):
                rgbt[which, c, here, place] = value
        return carry

    lax.fori_loop(0, rows // 8, strip, 0)
    kept[...] = rgbt[0]
    sent[...] = rgbt[1]


def merged_of(behind, held, got):
    mine = [held[c] for c in range(4)]
    theirs = [got[c] for c in range(4)]
    front = [jnp.where(behind, b, a) for a, b in zip(mine, theirs)]
    back = [jnp.where(behind, a, b) for a, b in zip(mine, theirs)]
    return [front[c] + front[3] * back[c] for c in range(3)] + [front[3] * back[3]]


def swap_body(bit_ref, held, got, kept, sent):
    width = kept.shape[2]
    values = merged_of(bit_ref[0] == 1, held, got)
    upper = bit_ref[1] == 1
    for c, value in enumerate(values):
        kept[c] = jnp.where(upper, value[:, width:], value[:, :width])
        sent[c] = jnp.where(upper, value[:, :width], value[:, width:])


def last_body(bit_ref, held, got, *rest):
    out = rest[-1]
    values = merged_of(bit_ref[0] == 1, held, got)
    for c in range(3):
        out[c] = values[c]
    out[3] = 1.0 - values[3]


def split_off(cells, bit):
    width = cells.shape[2] // 2
    low, high = cells[:, :, :width], cells[:, :, width:]
    return jnp.where(bit == 1, high, low), jnp.where(bit == 1, low, high)


def per_device(density, bins, colors, extinction, *, chunk_order, rows):
    layers, height, width = density.shape
    slabs = lax.axis_size("depth")
    tile_count = lax.axis_size("tile")
    scale = 0.6 / (layers * slabs)
    half = width // 2
    half_tiles = half // LANES
    slab = lax.axis_index("depth")
    rounds = slabs.bit_length() - 1
    bits = [jnp.right_shift(slab, r) & 1 for r in range(rounds)]
    side = bits[0]
    table = jnp.concatenate([colors, extinction[None, :]], 0).astype(jnp.float32)
    chunks = height // rows

    def along(array, axis, pairs):
        return lax.ppermute(array, axis, pairs)

    from_above = along(density[:, height - 1 :, :], "tile", [(i, i + 1) for i in range(tile_count - 1)])
    from_below = along(density[:, :1, :], "tile", [(i + 1, i) for i in range(tile_count - 1)])
    onward = [(i, i + 2) if i % 2 else (i, i - 2) for i in range(slabs)]
    onward = [(i, j) for i, j in onward if 0 <= j < slabs]
    backward = [(i, i - 2) if i % 2 else (i, i + 2) for i in range(slabs)]
    backward = [(i, j) for i, j in backward if 0 <= j < slabs]
    face = lax.dynamic_slice(density, (side * (layers - 1), 0, side * half), (1, height, half))[0]
    direct = along(face, "depth", onward)

    scalars = jnp.stack(bits[:2]).astype(jnp.int32)

    def whole(shape):
        return pl.BlockSpec(shape, lambda i, s: (0,) * len(shape))

    def edge_specs(chunk, half_of):
        if chunk == 0:
            first = (from_above, pl.BlockSpec((layers, 1, half), lambda i, s: (0, 0, half_of(s))), 0)
        else:
            first = (density, pl.BlockSpec((layers, 8, half), lambda i, s: (0, chunk * rows // 8 - 1, half_of(s))), 7)
        if chunk == chunks - 1:
            second = (from_below, pl.BlockSpec((layers, 1, half), lambda i, s: (0, 0, half_of(s))), 0)
        else:
            second = (density, pl.BlockSpec((layers, 8, half), lambda i, s: (0, (chunk + 1) * rows // 8, half_of(s))), 0)
        return first, second

    def pack(chunk):
        first, second = edge_specs(chunk, lambda s: 1 - s[0])
        block = pl.BlockSpec((layers, rows, half), lambda i, s: (0, chunk, 1 - s[0]))
        shape = (2 * layers * rows + 8, half)
        return pl.pallas_call(
            functools.partial(pack_body, layers, rows, first[2], second[2]),
            out_shape=jax.ShapeDtypeStruct(shape, jnp.float32),
            grid_spec=pltpu.PrefetchScalarGridSpec(
                num_scalar_prefetch=1,
                grid=(1,),
                in_specs=[
                    block,
                    first[1],
                    second[1],
                    pl.BlockSpec((layers, rows, LANES), lambda i, s: (0, chunk, half_tiles - 1 + s[0])),
                    block,
                ],
                out_specs=whole(shape),
            ),
            compiler_params=params(),
            cost_estimate=pl.CostEstimate(flops=0, bytes_accessed=4 * 4 * layers * rows * half, transcendentals=0),
            name="pack",
        )(scalars, density, first[0], second[0], density, bins)

    def render(chunk, message, passed):
        first, second = edge_specs(chunk, lambda s: s[0])
        block = pl.BlockSpec((layers, rows, half), lambda i, s: (0, chunk, s[0]))
        shape = (4, rows, half // 2)
        out = jax.ShapeDtypeStruct(shape, jnp.float32)
        deep = 2 * layers
        return pl.pallas_call(
            functools.partial(render_body, layers, rows, scale, first[2], second[2]),
            out_shape=(out, out),
            grid_spec=pltpu.PrefetchScalarGridSpec(
                num_scalar_prefetch=1,
                grid=(1,),
                in_specs=[
                    whole(table.shape),
                    block,
                    first[1],
                    second[1],
                    pl.BlockSpec((layers, rows, LANES), lambda i, s: (0, chunk, half_tiles - s[0])),
                    block,
                    whole(message.shape),
                    pl.BlockSpec((rows, half), lambda i, s: (chunk, 0)),
                    whole(passed.shape),
                ],
                out_specs=(whole(shape), whole(shape)),
                scratch_shapes=[
                    pltpu.VMEM((deep + 2, rows + 16, half), jnp.float32),
                    pltpu.VMEM((2, deep, rows, LANES), jnp.float32),
                    pltpu.VMEM((deep, rows, half), jnp.int32),
                    pltpu.VMEM((2, 4, rows, half // 2), jnp.float32),
                    pltpu.VMEM((8, 8, LANES), jnp.float32),
                ],
            ),
            compiler_params=params(),
            cost_estimate=pl.CostEstimate(flops=60 * deep * rows * half, bytes_accessed=40 * rows * half, transcendentals=deep * rows * half),
            name="render",
        )(scalars, table, density, first[0], second[0], density, bins, message, direct, passed)

    def small(body, scalars, ins, outs, out_spec=None, aliases=None, alias=None):
        specs = [whole(a.shape) for a in ins]
        operands = list(ins)
        if alias is not None:
            specs.append(pl.BlockSpec(memory_space=pl.ANY))
            operands.append(alias)
        return pl.pallas_call(
            body,
            out_shape=outs,
            grid_spec=pltpu.PrefetchScalarGridSpec(num_scalar_prefetch=1, grid=(1,), in_specs=specs, out_specs=out_spec),
            compiler_params=params(),
            input_output_aliases=aliases or {},
            cost_estimate=pl.CostEstimate(flops=8 * ins[0].size, bytes_accessed=16 * ins[0].size, transcendentals=0),
            name="merge",
        )(scalars, *operands)

    image = None
    parts = {}
    for chunk in chunk_order:
        message = along(pack(chunk), "depth", [(i, i ^ 1) for i in range(slabs)])
        layer = lax.dynamic_slice(message, ((1 - side) * (layers - 1) * rows, 0), (rows, half))
        passed = along(layer, "depth", backward)
        kept, sent = render(chunk, message, passed)
        for r in range(1, rounds):
            got = along(sent, "depth", [(i, i ^ (1 << r)) for i in range(slabs)])
            cols = kept.shape[2]
            if r == rounds - 1 and cols % LANES == 0:
                shape = (4, height, cols)
                image = small(
                    last_body,
                    bits[r][None],
                    [kept, got],
                    jax.ShapeDtypeStruct(shape, jnp.float32),
                    pl.BlockSpec((4, rows, cols), lambda i, s, chunk=chunk: (0, chunk, 0)),
                    {3: 0} if image is not None else None,
                    image,
                )
            elif r < rounds - 1 and cols % (2 * LANES) == 0:
                shape = (4, rows, cols // 2)
                out = jax.ShapeDtypeStruct(shape, jnp.float32)
                kept, sent = small(swap_body, jnp.stack([bits[r], bits[r + 1]]), [kept, got], (out, out), (whole(shape), whole(shape)))
            else:
                values = jnp.stack(merged_of(bits[r] == 1, kept, got))
                if r < rounds - 1:
                    kept, sent = split_off(values, bits[r + 1])
                else:
                    parts[chunk] = jnp.concatenate([values[:3], 1.0 - values[3:]], 0)
    if image is None:
        image = jnp.concatenate([parts[c] for c in range(chunks)], 1)
    return image


def solution(mesh):
    return jax.shard_map(
        functools.partial(per_device, chunk_order=(1, 2, 0, 3), rows=32),
        mesh=mesh,
        in_specs=(P("depth", "tile", None), P("depth", "tile", None), P(), P()),
        out_specs=P(None, "tile", "depth"),
        check_vma=False,
    )
```

```python
import functools

import jax
import jax.numpy as jnp
from jax import lax
from jax.experimental import pallas as pl
from jax.experimental.pallas import tpu as pltpu
from jax.sharding import PartitionSpec as P

LANES = 128
VMEM_LIMIT = 12 * 1024 * 1024
FLOPS_PER_US = 1.15e9


def seed_token(token):
    token[...] = jnp.zeros_like(token)


def edge_column(side, column, layers, rows):
    lane = lax.broadcasted_iota(jnp.int32, (8, LANES), 1)
    edges = jnp.zeros((8, LANES), jnp.float32)
    for layer in range(layers):
        for step in range(rows // 8):
            block = column(layer, step * 8)
            edge = jnp.where(side == 0, block[:, LANES - 1 :], block[:, :1])
            edges = jnp.where(lane == layer * (rows // 8) + step, edge, edges)
    return edges


def store_edges(out, base, edges):
    out[base + 4 : base + 8, :] = jnp.zeros((4, out.shape[1]), jnp.float32)
    out[base + 4 : base + 8, :LANES] = edges[:4]
    out[base + 4 : base + 8, LANES : 2 * LANES] = edges[4:]


def position():
    slab = lax.axis_index("depth")
    return lambda r: jnp.right_shift(slab, r) & 1


def start_all(pairs, sems):
    copies = [pltpu.make_async_copy(source, target, sems.at[n]) for n, (source, target) in enumerate(pairs)]
    for copy in copies:
        copy.start()
    return copies


def pack_body(start, rows, ranges, density, bins, *rest):
    out, token, entry, column, above, below, sems = rest[-7:]
    seed_token(token)
    side = position()(0)
    layers, height, width = density.shape
    half = width // 2
    theirs = pl.ds(pl.multiple_of((1 - side) * half, LANES), half)
    border = pl.ds(pl.multiple_of(half - LANES + side * LANES, LANES), LANES)
    pairs = [(bins.at[:, start : start + rows, theirs], entry)]
    base = 0
    for begin, size in ranges:
        pairs.append((density.at[side * (layers - 1), begin : begin + size, theirs], out.at[base : base + size, :]))
        base += size
    for layer in range(layers - 1):
        pairs.append((density.at[1 - side + layer, start : start + rows, theirs], out.at[base : base + rows, :]))
        base += rows
    pairs.append((density.at[:, start : start + rows, border], column))
    if start > 0:
        pairs.append((density.at[:, start - 8 : start, theirs], above))
    if start + rows < height:
        pairs.append((density.at[:, start + rows : start + rows + 8, theirs], below))
    copies = start_all(pairs, sems)
    for copy in copies:
        copy.wait()
    for layer in range(layers):
        out[base : base + rows, :] = entry[layer].astype(jnp.float32)
        base += rows
    for layer in range(layers):
        before = above[layer, 7:8, :] if start > 0 else rest[0][layer, 0:1, theirs]
        after = below[layer, 0:1, :] if start + rows < height else rest[1][layer, 0:1, theirs]
        out[base + 2 * layer : base + 2 * layer + 1, :] = before
        out[base + 2 * layer + 1 : base + 2 * layer + 2, :] = after
    store_edges(out, base, edge_column(side, lambda layer, row: column[layer, row : row + 8, :], layers, rows))


def packed_table(table, lookup):
    red, green, blue = ((table[c : c + 1, :] * 2048.0).astype(jnp.int32) for c in range(3))
    absorbed = (table[3:4, :] * 4096.0).astype(jnp.int32)
    for word, value in enumerate((red * 4096 + green, blue * 131072 + absorbed)):
        for part in range(2):
            lookup[2 * word + part] = jnp.broadcast_to(value[:, part * LANES : (part + 1) * LANES], (8, LANES))


def render_body(start, rows, skip, offset, scale, table, density, bins, direct, face, message, passed, *rest):
    kept, sent, token, cells, ends, entry, rgbt, lookup, sems = rest[-9:]
    seed_token(token)
    bits = position()
    side, bit = bits(0), bits(1)
    layers, height, width = density.shape
    half = width // 2
    tiles = half // LANES
    deep = 2 * layers
    inner = layers - 1
    mine = side * layers
    other = (1 - side) * layers
    ours = pl.ds(pl.multiple_of(side * half, LANES), half)
    border = pl.ds(pl.multiple_of(half - side * LANES, LANES), LANES)
    body = pl.ds(8, rows)
    top = max(start - 8, 0)
    bottom = min(start + rows + 8, height)
    copies = start_all(
        [
            (density.at[:, top:bottom, ours], cells.at[pl.ds(1 + mine, layers), pl.ds(8 + top - start, bottom - top), :]),
            (bins.at[:, start : start + rows, ours], entry.at[pl.ds(mine, layers)]),
            (density.at[:, start : start + rows, border], ends.at[1 - side, pl.ds(mine, layers)]),
            (direct.at[start : start + rows, :], cells.at[(1 - side) * (deep + 1), body, :]),
        ],
        sems,
    )
    packed_table(table, lookup)
    base = skip + (inner + layers) * rows
    cells[side * (deep + 1), body, :] = passed[offset : offset + rows, :]
    edges = jnp.concatenate([message[base + 4 : base + 8, :LANES], message[base + 4 : base + 8, LANES : 2 * LANES]], 0)
    ends[side] = jnp.zeros_like(ends[side])
    cells[1 + other + (1 - side) * inner, body, :] = face[offset : offset + rows, :]
    for layer in range(inner):
        cells[1 + other + side + layer, body, :] = message[skip + layer * rows : skip + (layer + 1) * rows, :]
    for layer in range(layers):
        if start == 0:
            cells[1 + mine + layer, 7:8, :] = rest[0][layer, 0:1, ours]
        if start + rows == height:
            cells[1 + mine + layer, 8 + rows : 9 + rows, :] = rest[1][layer, 0:1, ours]
        cells[1 + other + layer, 7:8, :] = message[base + 2 * layer : base + 2 * layer + 1, :]
        cells[1 + other + layer, 8 + rows : 9 + rows, :] = message[base + 2 * layer + 1 : base + 2 * layer + 2, :]
        entry[other + layer] = message[skip + (inner + layer) * rows : skip + (inner + layer + 1) * rows, :].astype(jnp.int32)
        for step in range(rows // 8):
            place = layer * (rows // 8) + step
            ends[1 - side, other + layer, step * 8 : step * 8 + 8, :] = jnp.broadcast_to(edges[:, place : place + 1], (8, LANES))
    for copy in copies:
        copy.wait()
    lane = lax.broadcasted_iota(jnp.int32, (8, LANES), 1)
    line = lax.broadcasted_iota(jnp.int32, (8, LANES), 0)

    def strip(step, carry):
        row = pl.multiple_of(step * 8, 8)
        here = pl.ds(row, 8)

        def tile_of(layer, tile):
            if tile < 0:
                return ends[0, layer, here, :]
            if tile == tiles:
                return ends[1, layer, here, :]
            return cells[1 + layer, pl.ds(row + 8, 8), tile * LANES : (tile + 1) * LANES]

        for tile in range(tiles):
            span = slice(tile * LANES, (tile + 1) * LANES)
            through = None
            total = None
            for layer in range(deep):
                before = cells[layer, pl.ds(row + 8, 8), span]
                after = cells[layer + 2, pl.ds(row + 8, 8), span]
                cell = tile_of(layer, tile)
                up = pltpu.roll(jnp.where(line == 7, cells[1 + layer, here, span], cell), 1, 0)
                down = pltpu.roll(jnp.where(line == 0, cells[1 + layer, pl.ds(row + 16, 8), span], cell), 7, 0)
                left = pltpu.roll(jnp.where(lane == LANES - 1, tile_of(layer, tile - 1), cell), 1, 1)
                right = pltpu.roll(jnp.where(lane == 0, tile_of(layer, tile + 1), cell), LANES - 1, 1)
                gx = after - before
                gy = down - up
                gz = right - left
                lit = jnp.abs((0.336 / 2048) * gx + (0.42 / 2048) * gy + (0.448 / 2048) * gz)
                shade = 0.3 / 2048 + lit * lax.rsqrt(gx * gx + gy * gy + gz * gz + 4.0)
                index = entry[layer, here, span]
                low_index = index & (LANES - 1)
                upper = index >= LANES
                words = []
                for word in range(2):
                    first = jnp.take_along_axis(lookup[2 * word], low_index, axis=1, mode="promise_in_bounds")
                    second = jnp.take_along_axis(lookup[2 * word + 1], low_index, axis=1, mode="promise_in_bounds")
                    words.append(jnp.where(upper, second, first))
                colour = [(words[0] >> 12).astype(jnp.float32), (words[0] & 4095).astype(jnp.float32), (words[1] >> 17).astype(jnp.float32)]
                passing = jnp.exp2((words[1] & 131071).astype(jnp.float32) * (-scale * 1.4426950408889634 / 4096))
                if layer == 0:
                    weight = shade * (1.0 - passing)
                    total = [weight * colour[c] for c in range(3)]
                    through = passing
                else:
                    weight = shade * (through * (1.0 - passing))
                    total = [total[c] + weight * colour[c] for c in range(3)]
                    through = through * passing
            which = jnp.where(bit == 0, tile // (tiles // 2), 1 - tile // (tiles // 2))
            place = slice((tile % (tiles // 2)) * LANES, (tile % (tiles // 2) + 1) * LANES)
            for c, value in enumerate(total + [through]):
                rgbt[which, c, here, place] = value
        return carry

    lax.fori_loop(0, rows // 8, strip, 0)
    kept[...] = rgbt[0]
    sent[...] = rgbt[1]


def merged_of(behind, held, got):
    mine = [held[c] for c in range(4)]
    theirs = [got[c] for c in range(4)]
    front = [jnp.where(behind, b, a) for a, b in zip(mine, theirs)]
    back = [jnp.where(behind, a, b) for a, b in zip(mine, theirs)]
    return [front[c] + front[3] * back[c] for c in range(3)] + [front[3] * back[3]]


def swap_body(count, joined, r, *rest):
    kept, sent, token = rest[-3:]
    seed_token(token)
    width = kept.shape[2]
    bits = position()
    upper = bits(r + 1) == 1
    row = 0
    for held, got in zip(rest[2 * count : 2 * count + joined], rest[2 * count + joined : 2 * count + 2 * joined]):
        rows = held.shape[1]
        kept[:, row : row + rows, :] = held[...]
        sent[:, row : row + rows, :] = got[...]
        row += rows
    for held, got in zip(rest[:count], rest[count : 2 * count]):
        rows = held.shape[1]
        for c, value in enumerate(merged_of(bits(r) == 1, held, got)):
            kept[c, row : row + rows, :] = jnp.where(upper, value[:, width:], value[:, :width])
            sent[c, row : row + rows, :] = jnp.where(upper, value[:, :width], value[:, width:])
        row += rows


def last_body(ranges, r, held, got, *rest):
    out, token, done, sems = rest[-4:]
    seed_token(token)
    values = merged_of(position()(r) == 1, held, got)
    for c in range(3):
        done[c] = values[c]
    done[3] = 1.0 - values[3]
    row = 0
    copies = []
    for number, (start, rows) in enumerate(ranges):
        copies.append(pltpu.make_async_copy(done.at[:, row : row + rows, :], out.at[:, start : start + rows, :], sems.at[number]))
        copies[-1].start()
        row += rows
    for copy in copies:
        copy.wait()


def split_off(cells, bit):
    width = cells.shape[2] // 2
    low, high = cells[:, :, :width], cells[:, :, width:]
    return jnp.where(bit == 1, high, low), jnp.where(bit == 1, low, high)


def per_device(density, bins, colors, extinction, *, chunks, steps, costs, far):
    volume = pltpu.with_memory_space_constraint(density, pltpu.HBM)
    entries = pltpu.with_memory_space_constraint(bins, pltpu.HBM)
    layers, height, width = density.shape
    slabs = lax.axis_size("depth")
    tile_count = lax.axis_size("tile")
    scale = 0.6 / (layers * slabs)
    half = width // 2
    deep = 2 * layers
    rounds = slabs.bit_length() - 1
    slab = lax.axis_index("depth")
    bits = [jnp.right_shift(slab, r) & 1 for r in range(rounds)]
    side = bits[0]
    table = jnp.concatenate([colors, extinction[None, :]], 0).astype(jnp.float32)
    swaps = [[(i, i ^ (1 << r)) for i in range(slabs)] for r in range(rounds)]
    onward = [(i, i + 2) if i % 2 else (i, i - 2) for i in range(slabs)]
    onward = [(i, j) for i, j in onward if 0 <= j < slabs]
    backward = [(i, i - 2) if i % 2 else (i, i + 2) for i in range(slabs)]
    backward = [(i, j) for i, j in backward if 0 <= j < slabs]
    vmem = pl.BlockSpec(memory_space=pltpu.VMEM)
    hbm = pl.BlockSpec(memory_space=pltpu.HBM)
    anywhere = pl.BlockSpec(memory_space=pl.ANY)
    last = []

    def call(body, operands, specs, outs, out_specs, name, micros, scratch=(), aliases=None):
        results = pl.pallas_call(
            body,
            out_shape=[*outs, jax.ShapeDtypeStruct((8, LANES), jnp.float32)],
            in_specs=[*specs, *[anywhere] * len(last)],
            out_specs=[*out_specs, vmem],
            scratch_shapes=scratch,
            compiler_params=pltpu.CompilerParams(vmem_limit_bytes=VMEM_LIMIT),
            input_output_aliases=aliases or {},
            cost_estimate=pl.CostEstimate(flops=int(micros * FLOPS_PER_US), bytes_accessed=1024, transcendentals=0),
            name=name,
        )(*operands, *last)
        last[:] = [results[-1]]
        return results[:-1]

    def after_last(array):
        return lax.optimization_barrier((array, *last))[0] if last else array

    messages = []
    faces = {}

    def send_message(number):
        start, rows, ranges = chunks[number]
        count = sum(size for _, size in ranges)
        shape = jax.ShapeDtypeStruct((count + (2 * layers - 1) * rows + 8, half), jnp.float32)
        scratch = [
            pltpu.VMEM((layers, rows, half), jnp.int32),
            pltpu.VMEM((layers, rows, LANES), jnp.float32),
            pltpu.VMEM((layers, 8, half), jnp.float32),
            pltpu.VMEM((layers, 8, half), jnp.float32),
            pltpu.SemaphoreType.DMA((len(ranges) + layers + 3,)),
        ]
        beyond = [from_above, from_below] if start == 0 or start + rows == height else []
        last.extend([from_above, from_below] if number == 2 else [])
        body = functools.partial(pack_body, start, rows, ranges)
        specs = [hbm, hbm] + [vmem] * len(beyond)
        packed = call(body, [*((volume, entries) if number < far else (density, bins)), *beyond], specs, [shape], [vmem], "pack", costs[0], scratch)[0]
        message = lax.ppermute(packed, "depth", swaps[0])
        messages.append(message)
        if ranges:
            passed = lax.ppermute(message[:count], "depth", backward)
            offset = 0
            for begin, size in ranges:
                faces[begin] = (offset, message, passed)
                offset += size

    def render(number):
        start, rows, ranges = chunks[number]
        offset, face, passed = faces[start]
        skip = sum(size for _, size in ranges)
        out = jax.ShapeDtypeStruct((4, rows, half // 2), jnp.float32)
        beyond = [from_above, from_below] if start == 0 or start + rows == height else []
        return call(
            functools.partial(render_body, start, rows, skip, offset, scale),
            [table, *((volume, entries) if far > 9 else (density, bins)), direct, face, messages[number], passed, *beyond],
            [vmem, hbm, hbm, anywhere, vmem, vmem, vmem] + [vmem] * len(beyond),
            [out, out],
            [vmem, vmem],
            "render",
            costs[1] * (0.3 + rows / 21),
            [
                pltpu.VMEM((deep + 2, rows + 16, half), jnp.float32),
                pltpu.VMEM((2, deep, rows, LANES), jnp.float32),
                pltpu.VMEM((deep, rows, half), jnp.int32),
                pltpu.VMEM((2, 4, rows, half // 2), jnp.float32),
                pltpu.VMEM((4, 8, LANES), jnp.int32),
                pltpu.SemaphoreType.DMA((4,)),
            ],
        )

    image = None
    parts = {}

    def land(entries, send=True, ready=()):
        nonlocal image
        r = entries[0][1]
        ranges = sum((entry[0] for entry in entries), [])
        kepts = [entry[2] for entry in entries]
        gots = [entry[3] for entry in entries]
        ranges = sum((entry[0] for entry in ready), []) + ranges
        rows = sum(size for _, size in ranges)
        cols = kepts[0].shape[2]
        if r == rounds - 1 and cols % LANES == 0:
            image = call(
                functools.partial(last_body, ranges, r),
                [kepts[0], gots[0]] + ([image] if image is not None else []),
                [vmem, vmem] + ([hbm] if image is not None else []),
                [jax.ShapeDtypeStruct((4, height, cols), jnp.float32)],
                [hbm],
                "finish",
                costs[3],
                [pltpu.VMEM((4, rows, cols), jnp.float32), pltpu.SemaphoreType.DMA((len(ranges),))],
                aliases={2: 0} if image is not None else None,
            )[0]
            return None
        if r < rounds - 1 and cols % (2 * LANES) == 0:
            out = jax.ShapeDtypeStruct((4, rows, cols // 2), jnp.float32)
            kept, sent = call(
                functools.partial(swap_body, len(entries), len(ready), r),
                [*kepts, *gots, *[entry[2] for entry in ready], *[entry[3] for entry in ready]],
                [vmem] * (2 * len(entries) + 2 * len(ready)),
                [out, out],
                [vmem, vmem],
                "merge",
                costs[2],
            )
        else:
            values = jnp.stack(merged_of(bits[r] == 1, jnp.concatenate(kepts, 1), jnp.concatenate(gots, 1)))
            if r == rounds - 1:
                values = jnp.concatenate([values[:3], 1.0 - values[3:]], 0)
                for start, size in ranges:
                    parts[start] = values[:, :size]
                    values = values[:, size:]
                return None
            kept, sent = split_off(values, bits[r + 1])
            kept, sent = (jnp.concatenate([*[entry[n] for entry in ready], part], 1) for n, part in ((2, kept), (3, sent)))
        if not send:
            return (ranges, r + 1, kept, sent)
        return (ranges, r + 1, kept, lax.ppermute(sent, "depth", swaps[r + 1]))

    flying = {}
    held = []
    for kind, number in steps:
        if kind == "pack":
            send_message(number)
        elif kind == "edges":
            near = after_last(density)
            from_above = lax.ppermute(near[:, height - 1 :, :], "tile", [(i, i + 1) for i in range(tile_count - 1)])
            from_below = lax.ppermute(near[:, :1, :], "tile", [(i + 1, i) for i in range(tile_count - 1)])
        elif kind == "outer":
            outer = lax.dynamic_slice(after_last(density), (side * (layers - 1), 0, side * half), (1, height, half))[0]
            direct = lax.ppermute(outer, "depth", onward)
        elif kind == "wait":
            last.extend([from_above, from_below])
        elif kind == "render":
            start, rows, _ = chunks[number]
            kept, sent = render(number)
            flying[number] = ([(start, rows)], 1, kept, lax.ppermute(sent, "depth", swaps[1]))
        elif kind == "keep":
            held.append(land([flying.pop(number)], send=False))
        else:
            flying[number] = land([flying[number]], ready=held if flying[number][1] < rounds - 1 else ())
            held = held if flying[number] is None else []
    while any(flying.values()):
        for number in list(flying):
            if flying[number]:
                flying[number] = land([flying[number]])
    if image is None:
        image = jnp.concatenate([parts[start] for start in sorted(parts)], 1)
    return image


def plan(height):
    unit = height // 16
    chunks = [(start * unit, rows * unit, [(s * unit, r * unit) for s, r in ranges]) for start, rows, ranges in [(2, 2, [(4, 4), (2, 2)]), (4, 4, [(8, 4), (12, 4), (0, 2)]), (8, 4, []), (12, 4, []), (0, 2, [])]]
    steps = ['p0', 'o0', 'p1', 'e0', 'p2', 'r0', 'p3', 'k0', 'r1', 'p4', 'r2', 'l1', 'r3', 'l2', 'r4', 'l1', 'l3', 'l2', 'l4', 'l3', 'l4']
    names = {"p": "pack", "r": "render", "l": "land", "e": "edges", "o": "outer", "w": "wait", "k": "keep"}
    return dict(far=1, costs=(0.4, 1.0, 0.1, 0.7), chunks=chunks, steps=[(names[s[0]], int(s[1:])) for s in steps])


def solution(mesh):
    def device(density, bins, colors, extinction):
        return per_device(density, bins, colors, extinction, **plan(density.shape[1]))

    return jax.shard_map(
        device,
        mesh=mesh,
        in_specs=(P("depth", "tile", None), P("depth", "tile", None), P(), P()),
        out_specs=P(None, "tile", "depth"),
        check_vma=False,
    )
```

```python
import functools

import jax
import jax.numpy as jnp
from jax import lax
from jax.experimental import pallas as pl
from jax.experimental.pallas import tpu as pltpu
from jax.sharding import PartitionSpec as P

LANES = 128
VMEM_LIMIT = 12 * 1024 * 1024
FLOPS_PER_US = 1.15e9


def seed_token(token):
    token[...] = jnp.zeros_like(token)


def edge_column(side, column, layers, rows):
    lane = lax.broadcasted_iota(jnp.int32, (8, LANES), 1)
    edges = jnp.zeros((8, LANES), jnp.float32)
    for layer in range(layers):
        for step in range(rows // 8):
            block = column(layer, step * 8)
            edge = jnp.where(side == 0, block[:, LANES - 1 :], block[:, :1])
            edges = jnp.where(lane == layer * (rows // 8) + step, edge, edges)
    return edges


def store_edges(out, base, edges):
    out[base + 4 : base + 8, :] = jnp.zeros((4, out.shape[1]), jnp.float32)
    out[base + 4 : base + 8, :LANES] = edges[:4]
    out[base + 4 : base + 8, LANES : 2 * LANES] = edges[4:]


def position():
    slab = lax.axis_index("depth")
    return lambda r: jnp.right_shift(slab, r) & 1


def start_all(pairs, sems):
    copies = [pltpu.make_async_copy(source, target, sems.at[n]) for n, (source, target) in enumerate(pairs)]
    for copy in copies:
        copy.start()
    return copies


def pack_body(start, rows, ranges, density, bins, *rest):
    out, token, entry, column, above, below, sems = rest[-7:]
    seed_token(token)
    side = position()(0)
    layers, height, width = density.shape
    half = width // 2
    theirs = pl.ds(pl.multiple_of((1 - side) * half, LANES), half)
    border = pl.ds(pl.multiple_of(half - LANES + side * LANES, LANES), LANES)
    pairs = [(bins.at[:, start : start + rows, theirs], entry)]
    base = 0
    for begin, size in ranges:
        pairs.append((density.at[side * (layers - 1), begin : begin + size, theirs], out.at[base : base + size, :]))
        base += size
    for layer in range(layers - 1):
        pairs.append((density.at[1 - side + layer, start : start + rows, theirs], out.at[base : base + rows, :]))
        base += rows
    pairs.append((density.at[:, start : start + rows, border], column))
    if start > 0:
        pairs.append((density.at[:, start - 8 : start, theirs], above))
    if start + rows < height:
        pairs.append((density.at[:, start + rows : start + rows + 8, theirs], below))
    copies = start_all(pairs, sems)
    for copy in copies:
        copy.wait()
    for layer in range(layers):
        out[base : base + rows, :] = entry[layer].astype(jnp.float32)
        base += rows
    for layer in range(layers):
        before = above[layer, 7:8, :] if start > 0 else rest[0][layer, 0:1, theirs]
        after = below[layer, 0:1, :] if start + rows < height else rest[1][layer, 0:1, theirs]
        out[base + 2 * layer : base + 2 * layer + 1, :] = before
        out[base + 2 * layer + 1 : base + 2 * layer + 2, :] = after
    store_edges(out, base, edge_column(side, lambda layer, row: column[layer, row : row + 8, :], layers, rows))


def packed_table(table, lookup):
    red, green, blue = ((table[c : c + 1, :] * 2048.0).astype(jnp.int32) for c in range(3))
    absorbed = (table[3:4, :] * 4096.0).astype(jnp.int32)
    for word, value in enumerate((red * 4096 + green, blue * 131072 + absorbed)):
        for part in range(2):
            lookup[2 * word + part] = jnp.broadcast_to(value[:, part * LANES : (part + 1) * LANES], (8, LANES))


def render_body(start, rows, skip, offset, scale, table, density, bins, direct, face, message, passed, *rest):
    kept, sent, token, cells, ends, entry, rgbt, lookup, sems = rest[-9:]
    seed_token(token)
    bits = position()
    side, bit = bits(0), bits(1)
    layers, height, width = density.shape
    half = width // 2
    tiles = half // LANES
    deep = 2 * layers
    inner = layers - 1
    mine = side * layers
    other = (1 - side) * layers
    ours = pl.ds(pl.multiple_of(side * half, LANES), half)
    border = pl.ds(pl.multiple_of(half - side * LANES, LANES), LANES)
    body = pl.ds(8, rows)
    top = max(start - 8, 0)
    bottom = min(start + rows + 8, height)
    copies = start_all(
        [
            (density.at[:, top:bottom, ours], cells.at[pl.ds(1 + mine, layers), pl.ds(8 + top - start, bottom - top), :]),
            (bins.at[:, start : start + rows, ours], entry.at[pl.ds(mine, layers)]),
            (density.at[:, start : start + rows, border], ends.at[1 - side, pl.ds(mine, layers)]),
            (direct.at[start : start + rows, :], cells.at[(1 - side) * (deep + 1), body, :]),
        ],
        sems,
    )
    packed_table(table, lookup)
    base = skip + (inner + layers) * rows
    cells[side * (deep + 1), body, :] = passed[offset : offset + rows, :]
    edges = jnp.concatenate([message[base + 4 : base + 8, :LANES], message[base + 4 : base + 8, LANES : 2 * LANES]], 0)
    ends[side] = jnp.zeros_like(ends[side])
    cells[1 + other + (1 - side) * inner, body, :] = face[offset : offset + rows, :]
    for layer in range(inner):
        cells[1 + other + side + layer, body, :] = message[skip + layer * rows : skip + (layer + 1) * rows, :]
    for layer in range(layers):
        if start == 0:
            cells[1 + mine + layer, 7:8, :] = rest[0][layer, 0:1, ours]
        if start + rows == height:
            cells[1 + mine + layer, 8 + rows : 9 + rows, :] = rest[1][layer, 0:1, ours]
        cells[1 + other + layer, 7:8, :] = message[base + 2 * layer : base + 2 * layer + 1, :]
        cells[1 + other + layer, 8 + rows : 9 + rows, :] = message[base + 2 * layer + 1 : base + 2 * layer + 2, :]
        entry[other + layer] = message[skip + (inner + layer) * rows : skip + (inner + layer + 1) * rows, :].astype(jnp.int32)
        for step in range(rows // 8):
            place = layer * (rows // 8) + step
            ends[1 - side, other + layer, step * 8 : step * 8 + 8, :] = jnp.broadcast_to(edges[:, place : place + 1], (8, LANES))
    for copy in copies:
        copy.wait()
    lane = lax.broadcasted_iota(jnp.int32, (8, LANES), 1)
    line = lax.broadcasted_iota(jnp.int32, (8, LANES), 0)

    def strip(step, carry):
        row = pl.multiple_of(step * 8, 8)
        here = pl.ds(row, 8)

        def tile_of(layer, tile):
            if tile < 0:
                return ends[0, layer, here, :]
            if tile == tiles:
                return ends[1, layer, here, :]
            return cells[1 + layer, pl.ds(row + 8, 8), tile * LANES : (tile + 1) * LANES]

        for tile in range(tiles):
            span = slice(tile * LANES, (tile + 1) * LANES)
            through = None
            total = None
            for layer in range(deep):
                before = cells[layer, pl.ds(row + 8, 8), span]
                after = cells[layer + 2, pl.ds(row + 8, 8), span]
                cell = tile_of(layer, tile)
                up = pltpu.roll(jnp.where(line == 7, cells[1 + layer, here, span], cell), 1, 0)
                down = pltpu.roll(jnp.where(line == 0, cells[1 + layer, pl.ds(row + 16, 8), span], cell), 7, 0)
                left = pltpu.roll(jnp.where(lane == LANES - 1, tile_of(layer, tile - 1), cell), 1, 1)
                right = pltpu.roll(jnp.where(lane == 0, tile_of(layer, tile + 1), cell), LANES - 1, 1)
                gx = after - before
                gy = down - up
                gz = right - left
                lit = jnp.abs((0.336 / 2048) * gx + (0.42 / 2048) * gy + (0.448 / 2048) * gz)
                shade = 0.3 / 2048 + lit * lax.rsqrt(gx * gx + gy * gy + gz * gz + 4.0)
                index = entry[layer, here, span]
                low_index = index & (LANES - 1)
                upper = index >= LANES
                words = []
                for word in range(2):
                    first = jnp.take_along_axis(lookup[2 * word], low_index, axis=1, mode="promise_in_bounds")
                    second = jnp.take_along_axis(lookup[2 * word + 1], low_index, axis=1, mode="promise_in_bounds")
                    words.append(jnp.where(upper, second, first))
                colour = [(words[0] >> 12).astype(jnp.float32), (words[0] & 4095).astype(jnp.float32), (words[1] >> 17).astype(jnp.float32)]
                passing = jnp.exp2((words[1] & 131071).astype(jnp.float32) * (-scale * 1.4426950408889634 / 4096))
                if layer == 0:
                    weight = shade * (1.0 - passing)
                    total = [weight * colour[c] for c in range(3)]
                    through = passing
                else:
                    weight = shade * (through * (1.0 - passing))
                    total = [total[c] + weight * colour[c] for c in range(3)]
                    through = through * passing
            which = jnp.where(bit == 0, tile // (tiles // 2), 1 - tile // (tiles // 2))
            place = slice((tile % (tiles // 2)) * LANES, (tile % (tiles // 2) + 1) * LANES)
            for c, value in enumerate(total + [through]):
                rgbt[which, c, here, place] = value
        return carry

    lax.fori_loop(0, rows // 8, strip, 0)
    kept[...] = rgbt[0]
    sent[...] = rgbt[1]


def merged_of(behind, held, got):
    mine = [held[c] for c in range(4)]
    theirs = [got[c] for c in range(4)]
    front = [jnp.where(behind, b, a) for a, b in zip(mine, theirs)]
    back = [jnp.where(behind, a, b) for a, b in zip(mine, theirs)]
    return [front[c] + front[3] * back[c] for c in range(3)] + [front[3] * back[3]]


def swap_body(count, joined, r, *rest):
    kept, sent, token = rest[-3:]
    seed_token(token)
    width = kept.shape[2]
    bits = position()
    upper = bits(r + 1) == 1
    row = 0
    for held, got in zip(rest[2 * count : 2 * count + joined], rest[2 * count + joined : 2 * count + 2 * joined]):
        rows = held.shape[1]
        kept[:, row : row + rows, :] = held[...]
        sent[:, row : row + rows, :] = got[...]
        row += rows
    for held, got in zip(rest[:count], rest[count : 2 * count]):
        rows = held.shape[1]
        for c, value in enumerate(merged_of(bits(r) == 1, held, got)):
            kept[c, row : row + rows, :] = jnp.where(upper, value[:, width:], value[:, :width])
            sent[c, row : row + rows, :] = jnp.where(upper, value[:, :width], value[:, width:])
        row += rows


def last_body(ranges, r, linked, held, got, *rest):
    out, token, done, sems = rest[-4:] if linked else (rest[-3], None, *rest[-2:])
    if linked:
        seed_token(token)
    values = merged_of(position()(r) == 1, held, got)
    for c in range(3):
        done[c] = values[c]
    done[3] = 1.0 - values[3]
    row = 0
    copies = []
    for number, (start, rows) in enumerate(ranges):
        copies.append(pltpu.make_async_copy(done.at[:, row : row + rows, :], out.at[:, start : start + rows, :], sems.at[number]))
        copies[-1].start()
        row += rows
    for copy in copies:
        copy.wait()


def split_off(cells, bit):
    width = cells.shape[2] // 2
    low, high = cells[:, :, :width], cells[:, :, width:]
    return jnp.where(bit == 1, high, low), jnp.where(bit == 1, low, high)


def per_device(density, bins, colors, extinction, *, chunks, steps, costs, far):
    volume = pltpu.with_memory_space_constraint(density, pltpu.HBM)
    entries = pltpu.with_memory_space_constraint(bins, pltpu.HBM)
    layers, height, width = density.shape
    slabs = lax.axis_size("depth")
    tile_count = lax.axis_size("tile")
    scale = 0.6 / (layers * slabs)
    half = width // 2
    deep = 2 * layers
    rounds = slabs.bit_length() - 1
    slab = lax.axis_index("depth")
    bits = [jnp.right_shift(slab, r) & 1 for r in range(rounds)]
    side = bits[0]
    table = jnp.concatenate([colors, extinction[None, :]], 0).astype(jnp.float32)
    swaps = [[(i, i ^ (1 << r)) for i in range(slabs)] for r in range(rounds)]
    onward = [(i, i + 2) if i % 2 else (i, i - 2) for i in range(slabs)]
    onward = [(i, j) for i, j in onward if 0 <= j < slabs]
    backward = [(i, i - 2) if i % 2 else (i, i + 2) for i in range(slabs)]
    backward = [(i, j) for i, j in backward if 0 <= j < slabs]
    vmem = pl.BlockSpec(memory_space=pltpu.VMEM)
    hbm = pl.BlockSpec(memory_space=pltpu.HBM)
    anywhere = pl.BlockSpec(memory_space=pl.ANY)
    last = []

    def call(body, operands, specs, outs, out_specs, name, micros, scratch=(), aliases=None, linked=True):
        results = pl.pallas_call(
            body,
            out_shape=[*outs, *[jax.ShapeDtypeStruct((8, LANES), jnp.float32)] * linked],
            in_specs=[*specs, *[anywhere] * len(last)],
            out_specs=[*out_specs, *[vmem] * linked],
            scratch_shapes=scratch,
            compiler_params=pltpu.CompilerParams(vmem_limit_bytes=VMEM_LIMIT),
            input_output_aliases=aliases or {},
            cost_estimate=pl.CostEstimate(flops=int(micros * FLOPS_PER_US), bytes_accessed=1024, transcendentals=0),
            name=name,
        )(*operands, *last)
        if not linked:
            return results
        last[:] = [results[-1]]
        return results[:-1]

    def after_last(array):
        return lax.optimization_barrier((array, *last))[0] if last else array

    messages = []
    faces = {}

    def send_message(number):
        start, rows, ranges = chunks[number]
        count = sum(size for _, size in ranges)
        shape = jax.ShapeDtypeStruct((count + (2 * layers - 1) * rows + 8, half), jnp.float32)
        scratch = [
            pltpu.VMEM((layers, rows, half), jnp.int32),
            pltpu.VMEM((layers, rows, LANES), jnp.float32),
            pltpu.VMEM((layers, 8, half), jnp.float32),
            pltpu.VMEM((layers, 8, half), jnp.float32),
            pltpu.SemaphoreType.DMA((len(ranges) + layers + 3,)),
        ]
        beyond = [from_above, from_below] if start == 0 or start + rows == height else []
        last.extend([from_above, from_below] if number == 2 else [])
        body = functools.partial(pack_body, start, rows, ranges)
        specs = [hbm, hbm] + [vmem] * len(beyond)
        packed = call(body, [*((volume, entries) if number < far else (density, bins)), *beyond], specs, [shape], [vmem], "pack", costs[0], scratch)[0]
        message = lax.ppermute(packed, "depth", swaps[0])
        messages.append(message)
        if ranges:
            passed = lax.ppermute(message[:count], "depth", backward)
            offset = 0
            for begin, size in ranges:
                faces[begin] = (offset, message, passed)
                offset += size

    def render(number):
        start, rows, ranges = chunks[number]
        offset, face, passed = faces[start]
        skip = sum(size for _, size in ranges)
        out = jax.ShapeDtypeStruct((4, rows, half // 2), jnp.float32)
        beyond = [from_above, from_below] if start == 0 or start + rows == height else []
        return call(
            functools.partial(render_body, start, rows, skip, offset, scale),
            [table, *((volume, entries) if far > 9 else (density, bins)), direct, face, messages[number], passed, *beyond],
            [vmem, hbm, hbm, anywhere, vmem, vmem, vmem] + [vmem] * len(beyond),
            [out, out],
            [vmem, vmem],
            "render",
            costs[1] * (0.3 + rows / 21),
            [
                pltpu.VMEM((deep + 2, rows + 16, half), jnp.float32),
                pltpu.VMEM((2, deep, rows, LANES), jnp.float32),
                pltpu.VMEM((deep, rows, half), jnp.int32),
                pltpu.VMEM((2, 4, rows, half // 2), jnp.float32),
                pltpu.VMEM((4, 8, LANES), jnp.int32),
                pltpu.SemaphoreType.DMA((4,)),
            ],
        )

    image = None
    parts = {}
    written = []

    def land(entries, send=True, ready=()):
        nonlocal image
        r = entries[0][1]
        ranges = sum((entry[0] for entry in entries), [])
        kepts = [entry[2] for entry in entries]
        gots = [entry[3] for entry in entries]
        ranges = sum((entry[0] for entry in ready), []) + ranges
        rows = sum(size for _, size in ranges)
        cols = kepts[0].shape[2]
        if r == rounds - 1 and cols % LANES == 0:
            written.extend(ranges)
            linked = len(written) < len(chunks)
            image = call(
                functools.partial(last_body, ranges, r, linked),
                [kepts[0], gots[0]] + ([image] if image is not None else []),
                [vmem, vmem] + ([hbm] if image is not None else []),
                [jax.ShapeDtypeStruct((4, height, cols), jnp.float32)],
                [hbm],
                "finish",
                costs[3],
                [pltpu.VMEM((4, rows, cols), jnp.float32), pltpu.SemaphoreType.DMA((len(ranges),))],
                aliases={2: 0} if image is not None else None,
                linked=linked,
            )[0]
            return None
        if r < rounds - 1 and cols % (2 * LANES) == 0:
            out = jax.ShapeDtypeStruct((4, rows, cols // 2), jnp.float32)
            kept, sent = call(
                functools.partial(swap_body, len(entries), len(ready), r),
                [*kepts, *gots, *[entry[2] for entry in ready], *[entry[3] for entry in ready]],
                [vmem] * (2 * len(entries) + 2 * len(ready)),
                [out, out],
                [vmem, vmem],
                "merge",
                costs[2],
            )
        else:
            values = jnp.stack(merged_of(bits[r] == 1, jnp.concatenate(kepts, 1), jnp.concatenate(gots, 1)))
            if r == rounds - 1:
                values = jnp.concatenate([values[:3], 1.0 - values[3:]], 0)
                for start, size in ranges:
                    parts[start] = values[:, :size]
                    values = values[:, size:]
                return None
            kept, sent = split_off(values, bits[r + 1])
            kept, sent = (jnp.concatenate([*[entry[n] for entry in ready], part], 1) for n, part in ((2, kept), (3, sent)))
        if not send:
            return (ranges, r + 1, kept, sent)
        return (ranges, r + 1, kept, lax.ppermute(sent, "depth", swaps[r + 1]))

    flying = {}
    held = []
    for kind, number in steps:
        if kind == "pack":
            send_message(number)
        elif kind == "edges":
            near = after_last(density)
            from_above = lax.ppermute(near[:, height - 1 :, :], "tile", [(i, i + 1) for i in range(tile_count - 1)])
            from_below = lax.ppermute(near[:, :1, :], "tile", [(i + 1, i) for i in range(tile_count - 1)])
        elif kind == "outer":
            outer = lax.dynamic_slice(after_last(density), (side * (layers - 1), 0, side * half), (1, height, half))[0]
            direct = lax.ppermute(outer, "depth", onward)
        elif kind == "wait":
            last.extend([from_above, from_below])
        elif kind == "render":
            start, rows, _ = chunks[number]
            kept, sent = render(number)
            flying[number] = ([(start, rows)], 1, kept, lax.ppermute(sent, "depth", swaps[1]))
        elif kind == "keep":
            held.append(land([flying.pop(number)], send=False))
        else:
            flying[number] = land([flying[number]], ready=held if flying[number][1] < rounds - 1 else ())
            held = held if flying[number] is None else []
    while any(flying.values()):
        for number in list(flying):
            if flying[number]:
                flying[number] = land([flying[number]])
    if image is None:
        image = jnp.concatenate([parts[start] for start in sorted(parts)], 1)
    return image


def plan(height):
    unit = height // 16
    chunks = [(start * unit, rows * unit, [(s * unit, r * unit) for s, r in ranges]) for start, rows, ranges in [(2, 3, [(2, 3), (5, 3)]), (5, 3, [(8, 4), (12, 4), (0, 2)]), (8, 4, []), (12, 4, []), (0, 2, [])]]
    steps = ['p0', 'o0', 'e0', 'p1', 'p2', 'p3', 'r0', 'k0', 'r1', 'p4', 'r2', 'l1', 'r3', 'l2', 'r4', 'l1', 'l3', 'l2', 'l4', 'l3', 'l4']
    names = {"p": "pack", "r": "render", "l": "land", "e": "edges", "o": "outer", "g": "across", "k": "keep"}
    return dict(far=1, costs=(0.52, 1.3, 0.13, 0.9099999999999999), chunks=chunks, steps=[(names[s[0]], int(s[1:])) for s in steps])


def solution(mesh):
    def device(density, bins, colors, extinction):
        return per_device(density, bins, colors, extinction, **plan(density.shape[1]))

    return jax.shard_map(
        device,
        mesh=mesh,
        in_specs=(P("depth", "tile", None), P("depth", "tile", None), P(), P()),
        out_specs=P(None, "tile", "depth"),
        check_vma=False,
    )
```

```python
import functools

import jax
import jax.numpy as jnp
from jax import lax
from jax.experimental import pallas as pl
from jax.experimental.pallas import tpu as pltpu
from jax.sharding import PartitionSpec as P

LANES = 128
VMEM_LIMIT = 12 * 1024 * 1024
FLOPS_PER_US = 1.15e9


def seed_token(token):
    token[...] = jnp.zeros_like(token)


def edge_column(side, column, layers, rows):
    lane = lax.broadcasted_iota(jnp.int32, (8, LANES), 1)
    edges = jnp.zeros((8, LANES), jnp.float32)
    for layer in range(layers):
        for step in range(rows // 8):
            block = column(layer, step * 8)
            edge = jnp.where(side == 0, block[:, LANES - 1 :], block[:, :1])
            edges = jnp.where(lane == layer * (rows // 8) + step, edge, edges)
    return edges


def store_edges(out, base, edges):
    out[base + 4 : base + 8, :] = jnp.zeros((4, out.shape[1]), jnp.float32)
    out[base + 4 : base + 8, :LANES] = edges[:4]
    out[base + 4 : base + 8, LANES : 2 * LANES] = edges[4:]


def position():
    slab = lax.axis_index("depth")
    return lambda r: jnp.right_shift(slab, r) & 1


def start_all(pairs, sems):
    copies = [pltpu.make_async_copy(source, target, sems.at[n]) for n, (source, target) in enumerate(pairs)]
    for copy in copies:
        copy.start()
    return copies


def pack_body(start, rows, ranges, density, bins, *rest):
    out, token, entry, column, above, below, sems = rest[-7:]
    seed_token(token)
    side = position()(0)
    layers, height, width = density.shape
    half = width // 2
    theirs = pl.ds(pl.multiple_of((1 - side) * half, LANES), half)
    border = pl.ds(pl.multiple_of(half - LANES + side * LANES, LANES), LANES)
    pairs = [(bins.at[:, start : start + rows, theirs], entry)]
    base = 0
    for begin, size in ranges:
        pairs.append((density.at[side * (layers - 1), begin : begin + size, theirs], out.at[base : base + size, :]))
        base += size
    for layer in range(layers - 1):
        pairs.append((density.at[1 - side + layer, start : start + rows, theirs], out.at[base : base + rows, :]))
        base += rows
    pairs.append((density.at[:, start : start + rows, border], column))
    if start > 0:
        pairs.append((density.at[:, start - 8 : start, theirs], above))
    if start + rows < height:
        pairs.append((density.at[:, start + rows : start + rows + 8, theirs], below))
    copies = start_all(pairs, sems)
    for copy in copies:
        copy.wait()
    for layer in range(layers):
        out[base : base + rows, :] = entry[layer].astype(jnp.float32)
        base += rows
    for layer in range(layers):
        before = above[layer, 7:8, :] if start > 0 else rest[0][layer, 0:1, theirs]
        after = below[layer, 0:1, :] if start + rows < height else rest[1][layer, 0:1, theirs]
        out[base + 2 * layer : base + 2 * layer + 1, :] = before
        out[base + 2 * layer + 1 : base + 2 * layer + 2, :] = after
    store_edges(out, base, edge_column(side, lambda layer, row: column[layer, row : row + 8, :], layers, rows))


def packed_table(table, lookup):
    red, green, blue = ((table[c : c + 1, :] * 2048.0).astype(jnp.int32) for c in range(3))
    absorbed = (table[3:4, :] * 4096.0).astype(jnp.int32)
    for word, value in enumerate((red * 4096 + green, blue * 131072 + absorbed)):
        for part in range(2):
            lookup[2 * word + part] = jnp.broadcast_to(value[:, part * LANES : (part + 1) * LANES], (8, LANES))


def render_body(start, rows, skip, offset, scale, table, density, bins, direct, face, message, passed, *rest):
    kept, sent, token, cells, ends, entry, rgbt, lookup, sems = rest[-9:]
    seed_token(token)
    bits = position()
    side, bit = bits(0), bits(1)
    layers, height, width = density.shape
    half = width // 2
    tiles = half // LANES
    deep = 2 * layers
    inner = layers - 1
    mine = side * layers
    other = (1 - side) * layers
    ours = pl.ds(pl.multiple_of(side * half, LANES), half)
    border = pl.ds(pl.multiple_of(half - side * LANES, LANES), LANES)
    body = pl.ds(8, rows)
    top = max(start - 8, 0)
    bottom = min(start + rows + 8, height)
    copies = start_all(
        [
            (density.at[:, top:bottom, ours], cells.at[pl.ds(1 + mine, layers), pl.ds(8 + top - start, bottom - top), :]),
            (bins.at[:, start : start + rows, ours], entry.at[pl.ds(mine, layers)]),
            (density.at[:, start : start + rows, border], ends.at[1 - side, pl.ds(mine, layers)]),
            (direct.at[start : start + rows, :], cells.at[(1 - side) * (deep + 1), body, :]),
        ],
        sems,
    )
    packed_table(table, lookup)
    base = skip + (inner + layers) * rows
    cells[side * (deep + 1), body, :] = passed[offset : offset + rows, :]
    edges = jnp.concatenate([message[base + 4 : base + 8, :LANES], message[base + 4 : base + 8, LANES : 2 * LANES]], 0)
    ends[side] = jnp.zeros_like(ends[side])
    cells[1 + other + (1 - side) * inner, body, :] = face[offset : offset + rows, :]
    for layer in range(inner):
        cells[1 + other + side + layer, body, :] = message[skip + layer * rows : skip + (layer + 1) * rows, :]
    for layer in range(layers):
        if start == 0:
            cells[1 + mine + layer, 7:8, :] = rest[0][layer, 0:1, ours]
        if start + rows == height:
            cells[1 + mine + layer, 8 + rows : 9 + rows, :] = rest[1][layer, 0:1, ours]
        cells[1 + other + layer, 7:8, :] = message[base + 2 * layer : base + 2 * layer + 1, :]
        cells[1 + other + layer, 8 + rows : 9 + rows, :] = message[base + 2 * layer + 1 : base + 2 * layer + 2, :]
        entry[other + layer] = message[skip + (inner + layer) * rows : skip + (inner + layer + 1) * rows, :].astype(jnp.int32)
        for step in range(rows // 8):
            place = layer * (rows // 8) + step
            ends[1 - side, other + layer, step * 8 : step * 8 + 8, :] = jnp.broadcast_to(edges[:, place : place + 1], (8, LANES))
    for copy in copies:
        copy.wait()
    lane = lax.broadcasted_iota(jnp.int32, (8, LANES), 1)
    line = lax.broadcasted_iota(jnp.int32, (8, LANES), 0)

    def strip(step, carry):
        row = pl.multiple_of(step * 8, 8)
        here = pl.ds(row, 8)

        def tile_of(layer, tile):
            if tile < 0:
                return ends[0, layer, here, :]
            if tile == tiles:
                return ends[1, layer, here, :]
            return cells[1 + layer, pl.ds(row + 8, 8), tile * LANES : (tile + 1) * LANES]

        for tile in range(tiles):
            span = slice(tile * LANES, (tile + 1) * LANES)
            through = None
            total = None
            for layer in range(deep):
                before = cells[layer, pl.ds(row + 8, 8), span]
                after = cells[layer + 2, pl.ds(row + 8, 8), span]
                cell = tile_of(layer, tile)
                up = pltpu.roll(jnp.where(line == 7, cells[1 + layer, here, span], cell), 1, 0)
                down = pltpu.roll(jnp.where(line == 0, cells[1 + layer, pl.ds(row + 16, 8), span], cell), 7, 0)
                left = pltpu.roll(jnp.where(lane == LANES - 1, tile_of(layer, tile - 1), cell), 1, 1)
                right = pltpu.roll(jnp.where(lane == 0, tile_of(layer, tile + 1), cell), LANES - 1, 1)
                gx = after - before
                gy = down - up
                gz = right - left
                lit = jnp.abs((0.336 / 2048) * gx + (0.42 / 2048) * gy + (0.448 / 2048) * gz)
                shade = 0.3 / 2048 + lit * lax.rsqrt(gx * gx + gy * gy + gz * gz + 4.0)
                index = entry[layer, here, span]
                low_index = index & (LANES - 1)
                upper = index >= LANES
                words = []
                for word in range(2):
                    first = jnp.take_along_axis(lookup[2 * word], low_index, axis=1, mode="promise_in_bounds")
                    second = jnp.take_along_axis(lookup[2 * word + 1], low_index, axis=1, mode="promise_in_bounds")
                    words.append(jnp.where(upper, second, first))
                colour = [(words[0] >> 12).astype(jnp.float32), (words[0] & 4095).astype(jnp.float32), (words[1] >> 17).astype(jnp.float32)]
                passing = jnp.exp2((words[1] & 131071).astype(jnp.float32) * (-scale * 1.4426950408889634 / 4096))
                if layer == 0:
                    weight = shade * (1.0 - passing)
                    total = [weight * colour[c] for c in range(3)]
                    through = passing
                else:
                    weight = shade * (through * (1.0 - passing))
                    total = [total[c] + weight * colour[c] for c in range(3)]
                    through = through * passing
            which = jnp.where(bit == 0, tile // (tiles // 2), 1 - tile // (tiles // 2))
            place = slice((tile % (tiles // 2)) * LANES, (tile % (tiles // 2) + 1) * LANES)
            for c, value in enumerate(total + [through]):
                rgbt[which, c, here, place] = value
        return carry

    lax.fori_loop(0, rows // 8, strip, 0, unroll=True)
    kept[...] = rgbt[0]
    sent[...] = rgbt[1]


def merged_of(behind, held, got):
    mine = [held[c] for c in range(4)]
    theirs = [got[c] for c in range(4)]
    front = [jnp.where(behind, b, a) for a, b in zip(mine, theirs)]
    back = [jnp.where(behind, a, b) for a, b in zip(mine, theirs)]
    return [front[c] + front[3] * back[c] for c in range(3)] + [front[3] * back[3]]


def swap_body(count, joined, r, *rest):
    kept, sent, token = rest[-3:]
    seed_token(token)
    width = kept.shape[2]
    bits = position()
    upper = bits(r + 1) == 1
    row = 0
    for held, got in zip(rest[2 * count : 2 * count + joined], rest[2 * count + joined : 2 * count + 2 * joined]):
        rows = held.shape[1]
        kept[:, row : row + rows, :] = held[...]
        sent[:, row : row + rows, :] = got[...]
        row += rows
    for held, got in zip(rest[:count], rest[count : 2 * count]):
        rows = held.shape[1]
        for c, value in enumerate(merged_of(bits(r) == 1, held, got)):
            kept[c, row : row + rows, :] = jnp.where(upper, value[:, width:], value[:, :width])
            sent[c, row : row + rows, :] = jnp.where(upper, value[:, :width], value[:, width:])
        row += rows


def last_body(ranges, r, linked, held, got, *rest):
    out, token, done, sems = rest[-4:] if linked else (rest[-3], None, *rest[-2:])
    if linked:
        seed_token(token)
    values = merged_of(position()(r) == 1, held, got)
    for c in range(3):
        done[c] = values[c]
    done[3] = 1.0 - values[3]
    row = 0
    copies = []
    for number, (start, rows) in enumerate(ranges):
        copies.append(pltpu.make_async_copy(done.at[:, row : row + rows, :], out.at[:, start : start + rows, :], sems.at[number]))
        copies[-1].start()
        row += rows
    for copy in copies:
        copy.wait()


def split_off(cells, bit):
    width = cells.shape[2] // 2
    low, high = cells[:, :, :width], cells[:, :, width:]
    return jnp.where(bit == 1, high, low), jnp.where(bit == 1, low, high)


def per_device(density, bins, colors, extinction, *, chunks, steps, costs, far):
    volume = pltpu.with_memory_space_constraint(density, pltpu.HBM)
    entries = pltpu.with_memory_space_constraint(bins, pltpu.HBM)
    layers, height, width = density.shape
    slabs = lax.axis_size("depth")
    tile_count = lax.axis_size("tile")
    scale = 0.6 / (layers * slabs)
    half = width // 2
    deep = 2 * layers
    rounds = slabs.bit_length() - 1
    slab = lax.axis_index("depth")
    bits = [jnp.right_shift(slab, r) & 1 for r in range(rounds)]
    side = bits[0]
    table = jnp.concatenate([colors, extinction[None, :]], 0).astype(jnp.float32)
    swaps = [[(i, i ^ (1 << r)) for i in range(slabs)] for r in range(rounds)]
    onward = [(i, i + 2) if i % 2 else (i, i - 2) for i in range(slabs)]
    onward = [(i, j) for i, j in onward if 0 <= j < slabs]
    backward = [(i, i - 2) if i % 2 else (i, i + 2) for i in range(slabs)]
    backward = [(i, j) for i, j in backward if 0 <= j < slabs]
    vmem = pl.BlockSpec(memory_space=pltpu.VMEM)
    hbm = pl.BlockSpec(memory_space=pltpu.HBM)
    anywhere = pl.BlockSpec(memory_space=pl.ANY)
    last = []

    def call(body, operands, specs, outs, out_specs, name, micros, scratch=(), aliases=None, linked=True):
        results = pl.pallas_call(
            body,
            out_shape=[*outs, *[jax.ShapeDtypeStruct((8, LANES), jnp.float32)] * linked],
            in_specs=[*specs, *[anywhere] * len(last)],
            out_specs=[*out_specs, *[vmem] * linked],
            scratch_shapes=scratch,
            compiler_params=pltpu.CompilerParams(vmem_limit_bytes=VMEM_LIMIT),
            input_output_aliases=aliases or {},
            cost_estimate=pl.CostEstimate(flops=int(micros * FLOPS_PER_US), bytes_accessed=1024, transcendentals=0),
            name=name,
        )(*operands, *last)
        if not linked:
            return results
        last[:] = [results[-1]]
        return results[:-1]

    def after_last(array):
        return lax.optimization_barrier((array, *last))[0] if last else array

    messages = []
    faces = {}

    def send_message(number):
        start, rows, ranges = chunks[number]
        count = sum(size for _, size in ranges)
        shape = jax.ShapeDtypeStruct((count + (2 * layers - 1) * rows + 8, half), jnp.float32)
        scratch = [
            pltpu.VMEM((layers, rows, half), jnp.int32),
            pltpu.VMEM((layers, rows, LANES), jnp.float32),
            pltpu.VMEM((layers, 8, half), jnp.float32),
            pltpu.VMEM((layers, 8, half), jnp.float32),
            pltpu.SemaphoreType.DMA((len(ranges) + layers + 3,)),
        ]
        beyond = [from_above, from_below] if start == 0 or start + rows == height else []
        last.extend([from_above, from_below] if number == 2 else [])
        body = functools.partial(pack_body, start, rows, ranges)
        specs = [hbm, hbm] + [vmem] * len(beyond)
        packed = call(body, [*((volume, entries) if number < far else (density, bins)), *beyond], specs, [shape], [vmem], "pack", costs[0], scratch)[0]
        message = lax.ppermute(packed, "depth", swaps[0])
        messages.append(message)
        if ranges:
            passed = lax.ppermute(message[:count], "depth", backward)
            offset = 0
            for begin, size in ranges:
                faces[begin] = (offset, message, passed)
                offset += size

    def render(number):
        start, rows, ranges = chunks[number]
        offset, face, passed = faces[start]
        skip = sum(size for _, size in ranges)
        out = jax.ShapeDtypeStruct((4, rows, half // 2), jnp.float32)
        beyond = [from_above, from_below] if start == 0 or start + rows == height else []
        return call(
            functools.partial(render_body, start, rows, skip, offset, scale),
            [table, *((volume, entries) if far > 9 else (density, bins)), direct, face, messages[number], passed, *beyond],
            [vmem, hbm, hbm, anywhere, vmem, vmem, vmem] + [vmem] * len(beyond),
            [out, out],
            [vmem, vmem],
            "render",
            costs[1] * (0.3 + rows / 21),
            [
                pltpu.VMEM((deep + 2, rows + 16, half), jnp.float32),
                pltpu.VMEM((2, deep, rows, LANES), jnp.float32),
                pltpu.VMEM((deep, rows, half), jnp.int32),
                pltpu.VMEM((2, 4, rows, half // 2), jnp.float32),
                pltpu.VMEM((4, 8, LANES), jnp.int32),
                pltpu.SemaphoreType.DMA((4,)),
            ],
        )

    image = None
    parts = {}
    written = []

    def land(entries, send=True, ready=()):
        nonlocal image
        r = entries[0][1]
        ranges = sum((entry[0] for entry in entries), [])
        kepts = [entry[2] for entry in entries]
        gots = [entry[3] for entry in entries]
        ranges = sum((entry[0] for entry in ready), []) + ranges
        rows = sum(size for _, size in ranges)
        cols = kepts[0].shape[2]
        if r == rounds - 1 and cols % LANES == 0:
            written.extend(ranges)
            linked = len(written) < len(chunks)
            image = call(
                functools.partial(last_body, ranges, r, linked),
                [kepts[0], gots[0]] + ([image] if image is not None else []),
                [vmem, vmem] + ([hbm] if image is not None else []),
                [jax.ShapeDtypeStruct((4, height, cols), jnp.float32)],
                [hbm],
                "finish",
                costs[3],
                [pltpu.VMEM((4, rows, cols), jnp.float32), pltpu.SemaphoreType.DMA((len(ranges),))],
                aliases={2: 0} if image is not None else None,
                linked=linked,
            )[0]
            return None
        if r < rounds - 1 and cols % (2 * LANES) == 0:
            out = jax.ShapeDtypeStruct((4, rows, cols // 2), jnp.float32)
            kept, sent = call(
                functools.partial(swap_body, len(entries), len(ready), r),
                [*kepts, *gots, *[entry[2] for entry in ready], *[entry[3] for entry in ready]],
                [vmem] * (2 * len(entries) + 2 * len(ready)),
                [out, out],
                [vmem, vmem],
                "merge",
                costs[2],
            )
        else:
            values = jnp.stack(merged_of(bits[r] == 1, jnp.concatenate(kepts, 1), jnp.concatenate(gots, 1)))
            if r == rounds - 1:
                values = jnp.concatenate([values[:3], 1.0 - values[3:]], 0)
                for start, size in ranges:
                    parts[start] = values[:, :size]
                    values = values[:, size:]
                return None
            kept, sent = split_off(values, bits[r + 1])
            kept, sent = (jnp.concatenate([*[entry[n] for entry in ready], part], 1) for n, part in ((2, kept), (3, sent)))
        if not send:
            return (ranges, r + 1, kept, sent)
        return (ranges, r + 1, kept, lax.ppermute(sent, "depth", swaps[r + 1]))

    flying = {}
    held = []
    for kind, number in steps:
        if kind == "pack":
            send_message(number)
        elif kind == "edges":
            near = after_last(density)
            from_above = lax.ppermute(near[:, height - 1 :, :], "tile", [(i, i + 1) for i in range(tile_count - 1)])
            from_below = lax.ppermute(near[:, :1, :], "tile", [(i + 1, i) for i in range(tile_count - 1)])
        elif kind == "outer":
            outer = lax.dynamic_slice(after_last(density), (side * (layers - 1), 0, side * half), (1, height, half))[0]
            direct = lax.ppermute(outer, "depth", onward)
        elif kind == "wait":
            last.extend([from_above, from_below])
        elif kind == "render":
            start, rows, _ = chunks[number]
            kept, sent = render(number)
            flying[number] = ([(start, rows)], 1, kept, lax.ppermute(sent, "depth", swaps[1]))
        elif kind == "keep":
            held.append(land([flying.pop(number)], send=False))
        else:
            flying[number] = land([flying[number]], ready=held if flying[number][1] < rounds - 1 else ())
            held = held if flying[number] is None else []
    while any(flying.values()):
        for number in list(flying):
            if flying[number]:
                flying[number] = land([flying[number]])
    if image is None:
        image = jnp.concatenate([parts[start] for start in sorted(parts)], 1)
    return image


def plan(height):
    unit = height // 16
    chunks = [(start * unit, rows * unit, [(s * unit, r * unit) for s, r in ranges]) for start, rows, ranges in [(2, 3, [(2, 3), (5, 3)]), (5, 3, [(8, 4), (12, 4), (0, 2)]), (8, 4, []), (12, 4, []), (0, 2, [])]]
    steps = ['p0', 'o0', 'e0', 'p1', 'p2', 'p3', 'r0', 'k0', 'r1', 'p4', 'r2', 'l1', 'r3', 'l2', 'r4', 'l1', 'l3', 'l2', 'l4', 'l3', 'l4']
    names = {"p": "pack", "r": "render", "l": "land", "e": "edges", "o": "outer", "g": "across", "k": "keep"}
    return dict(far=1, costs=(0.52, 1.3, 0.13, 0.9099999999999999), chunks=chunks, steps=[(names[s[0]], int(s[1:])) for s in steps])


def solution(mesh):
    def device(density, bins, colors, extinction):
        return per_device(density, bins, colors, extinction, **plan(density.shape[1]))

    return jax.shard_map(
        device,
        mesh=mesh,
        in_specs=(P("depth", "tile", None), P("depth", "tile", None), P(), P()),
        out_specs=P(None, "tile", "depth"),
        check_vma=False,
    )
```
